32 devices in a mesh: groups: 2 (over x), expert: 16 (over z, y, core).
Axes of the slice: x: 2, y: 2, z: 4, core: 2. Of those that a mesh axis runs over, the one named last changes fastest.
Arguments:
- residual: bfloat16 [4096, 3584], P(('groups', 'expert')), parts along dimension 0, may hold values from -24 to 24
- norm_gain: float32 [3584], replicated, may hold values from 0.25 to 1.75
- router: bfloat16 [3584, 4], replicated, may hold values from -0.09375 to 0.09375
- w_gate: bfloat16 [3584, 4096], P(None, 'expert'), may hold values from -0.09375 to 0.09375
- w_up: bfloat16 [3584, 4096], P(None, 'expert'), may hold values from -0.09375 to 0.09375
- w_down: bfloat16 [4096, 3584], P('expert'), may hold values from -0.1875 to 0.1875
- expert_ids: int32 [4096, 2], P(('groups', 'expert')), parts along dimension 0, may hold values from 0 to 3, all different within a row; in each aligned block of 128 rows (0 to 127, 128 to 255, ...) at most 96 rows name the same one
Outputs:
- layer_out: bfloat16 [4096, 3584], P(('groups', 'expert')), parts along dimension 0
The draws below stay inside these ranges and needn't reach their ends.
There are 2 independent parts, one for each index of `groups`. The reference program is written for one: setup_inputs(seed, part) draws one part's arguments, and reference() takes and returns one part's arrays. A program takes and returns all parts, laid end to end along the dimension named above; an argument that names none is the same for every part. Nothing has to cross between parts.
Inputs may be any that keep to these rules, and one draw needn't show every extreme that they name: `expert_ids`: each row names 2 different experts. Within the rows of one device no expert is named by more than 96 rows, and in every draw some device's rows name some expert exactly 96 times.
All inputs are finite; a program needn't handle non-finite values.
Results may differ from the reference program's by a relative error of at most 0.0054.
Values may be sent and summed in bfloat16 or wider, within the bound.
No kernel may reach another device: no remote copies, remote signals or barrier semaphores. Data moves between devices by JAX's collectives and lax.ppermute only.
A program may use at most 128 MiB of HBM per device.

```python
import math
import jax
import jax.numpy as jnp
import numpy as np
from jax import lax

D = 3584
FF_E = 1024
SPAN = 4
TOP = 2
TOK_DEV = 128
HID = 256
EXPERTS = 4
TOKENS = 2048
CAP = 96
N_EXPERT = 16


def draw_residual(key, part):
    noise_key = jax.random.fold_in(key, 11)
    column_key = jax.random.fold_in(key, 12)
    row_key = jax.random.fold_in(key, 13)
    column_scale = jnp.exp(jax.random.uniform(column_key, (1, D), jnp.float32, math.log(0.3), math.log(3.0)))
    row_scale = jnp.exp(jax.random.uniform(row_key, (TOKENS, 1), jnp.float32, math.log(0.5), math.log(2.0)))
    base_values = jnp.clip(jax.random.normal(noise_key, (TOKENS, D), jnp.float32), -4.0, 4.0)
    return (base_values * column_scale * row_scale).astype(jnp.bfloat16)


def shard_levels(stream_key, extent, cuts, low, top_value):
    gain, own = 1.0, jax.random.fold_in(stream_key, 6)
    for axis_at, blocks in cuts:
        steps = jnp.exp(jax.random.uniform(jax.random.fold_in(own, axis_at), (blocks,), jnp.float32, low / len(cuts), top_value / len(cuts)))
        gain = gain * jnp.repeat(steps, extent[axis_at] // blocks).reshape([-1 if axis == axis_at else 1 for axis in range(len(extent))])
    return gain


def deal_out(rng, own, number, rows, amount, top, most, skew):
    sequence = jax.random.permutation(rng, amount)
    packed, usual = shares(amount, rows * top, most, skew, True), shares(amount, rows * top, most, skew, False)
    places = jnp.arange(amount)

    def named(tallies, rotation):
        used = int((tallies > 0).sum())
        fixed = max(1, used // 4)
        shifted = fixed + (places - fixed + rotation * (used - fixed)) % max(1, amount - fixed)
        return jnp.zeros((amount,), jnp.int32).at[sequence[jnp.where(places < fixed, places, shifted)]].set(jnp.asarray(tallies, jnp.int32))

    tallies = jnp.where(number % 4 == 0, named(packed, number // 4), named(usual, number - number // 4 - 1))
    mixed = jax.random.permutation(jax.random.fold_in(own, 3), amount)
    giver, receiver = mixed[0:amount // 2 * 2:2], mixed[1:amount // 2 * 2:2]
    margin = jnp.minimum(tallies[giver] - 1, most - tallies[receiver]) // 2
    margin = jnp.where((giver == sequence[0]) | (receiver == sequence[0]) | (tallies[receiver] == 0), 0, jnp.maximum(margin, 0))
    shifted = jax.random.randint(jax.random.fold_in(own, 4), (amount // 2,), 0, 1 << 20) % (margin + 1)
    tallies = tallies.at[giver].add(-shifted).at[receiver].add(shifted)
    items = jnp.searchsorted(jnp.cumsum(tallies), jnp.arange(rows * top), side="right").astype(jnp.int32)
    table = items.reshape(top, rows).T
    table = table[jax.random.permutation(jax.random.fold_in(own, 1), rows)]
    rotation = jax.random.randint(jax.random.fold_in(own, 2), (rows, 1), 0, top)
    return jnp.take_along_axis(table, (jnp.arange(top)[None, :] + rotation) % top, axis=1)


def shares(count, total, reach, slope, full):
    portions = [(1 << 20) // math.isqrt(rank ** slope) + 1 for rank in range(1, count + 1)]
    largest = reach if full else min(reach, max(-(-total // count), total * portions[0] // sum(portions)))
    least = 1 if total - largest >= count - 1 else 0
    counts, spare = [largest] + [least] * (count - 1), total - largest - least * (count - 1)
    while spare > 0:
        free = [i for i in range(1, count) if counts[i] < largest] or [i for i in range(1, count) if counts[i] < reach]
        mass, remaining = sum([portions[i] for i in free]), spare
        for i in free:
            addition = min(reach - counts[i], max(1, remaining * portions[i] // mass), spare)
            counts[i] = counts[i] + addition
            spare = spare - addition
    return np.array(counts)


def scatter_about(stream_key, dims, spread, most, cuts=(), held_as=jnp.bfloat16):
    result = spread * jax.random.normal(stream_key, dims, jnp.float32)
    if cuts:
        result = result * shard_levels(stream_key, dims, cuts, -0.22, 0.18)
    return jnp.clip(result, -most, most).astype(held_as)


def setup_inputs(seed: int = 0, part: int = 0) -> dict:
    keys = jax.random.split(jax.random.key(seed), 8)
    own_keys = jax.random.split(jax.random.fold_in(keys[7], part), 8)
    residual = draw_residual(jax.random.fold_in(jax.random.fold_in(keys[7], part), 71), part)
    norm_gain = jnp.clip(1.0 + 0.15 * jax.random.normal(keys[1], (D,), jnp.float32), 0.25, 1.75)
    router = scatter_about(keys[2], (D, EXPERTS), D ** -0.5, 0.09375)
    w_gate = scatter_about(keys[3], (D, EXPERTS * FF_E), D ** -0.5, 0.09375, ((1, 16),))
    w_up = scatter_about(keys[4], (D, EXPERTS * FF_E), D ** -0.5, 0.09375, ((1, 16),))
    w_down = scatter_about(keys[5], (EXPERTS * FF_E, D), FF_E ** -0.5, 0.1875, ((0, 16),))
    expert_ids_keys = jax.random.split(jax.random.fold_in(own_keys[6], 1), TOKENS // TOK_DEV)
    expert_ids_turns = jax.random.permutation(jax.random.fold_in(own_keys[6], 3), TOKENS // TOK_DEV)
    expert_ids = jax.vmap(lambda own, number: deal_out(jax.random.fold_in(own_keys[6], 2), own, number, TOK_DEV, EXPERTS, TOP, CAP, 2))(expert_ids_keys, expert_ids_turns).reshape((TOKENS, TOP))
    return dict(residual=residual, norm_gain=norm_gain, router=router, w_gate=w_gate, w_up=w_up, w_down=w_down, expert_ids=expert_ids)


route_scale = 2.5
norm_eps = 1e-06

def normalize(residual, norm_gain):
    residual_wide = residual.astype(jnp.float32)
    mean_square = lax.optimization_barrier(jnp.mean(residual_wide * residual_wide, axis=1, keepdims=True))
    normed = (residual_wide * lax.rsqrt(mean_square + norm_eps) * norm_gain).astype(jnp.bfloat16)
    return (residual_wide, normed)

def routing(normed, router, expert_ids):
    logits = jnp.dot(normed, router, preferred_element_type=jnp.float32)
    affinity = jax.nn.sigmoid(logits)
    picked = expert_ids[:, :, None] == lax.iota(jnp.int32, router.shape[1])[None, None, :]
    chosen = lax.optimization_barrier(jnp.sum(jnp.where(picked, affinity[:, None, :], 0.0), axis=2))
    gate_values = route_scale * chosen / lax.optimization_barrier(jnp.sum(chosen, axis=1, keepdims=True))
    return (picked, gate_values)

def slot_numbers(picked, block_rows):
    total_rows, top_count, expert_count = picked.shape
    flat_pick = picked.reshape(total_rows // block_rows, block_rows * top_count, expert_count).astype(jnp.int32)
    before = jnp.cumsum(flat_pick, axis=1) - flat_pick
    return lax.optimization_barrier(jnp.sum(before * flat_pick, axis=2)).reshape(total_rows, top_count)

def reference(residual, norm_gain, router, w_gate, w_up, w_down, expert_ids):
    residual_wide, normed = normalize(residual, norm_gain)
    picked, gate_values = routing(normed, router, expert_ids)
    slot_index = slot_numbers(picked, TOK_DEV)
    block_index = lax.iota(jnp.int32, TOKENS) // TOK_DEV
    position = (block_index[:, None] * CAP + slot_index).astype(jnp.int32)
    owner_row = jnp.broadcast_to(lax.iota(jnp.int32, TOKENS)[:, None], (TOKENS, TOP))
    row_table = jnp.zeros((EXPERTS, N_EXPERT * CAP), jnp.int32).at[expert_ids, position].set(owner_row)
    filled = jnp.zeros((EXPERTS, N_EXPERT * CAP), jnp.int32).at[expert_ids, position].set(1)

    def one_expert(accumulated, expert):
        routed_rows = jnp.take(normed, row_table[expert], axis=0)
        routed_rows = jnp.where(filled[expert][:, None] > 0, routed_rows, jnp.zeros_like(routed_rows))
        summed = jnp.zeros((N_EXPERT * CAP, D), jnp.float32)
        for member in range(SPAN):
            column_start = (expert * SPAN + member) * HID
            gate_proj = jnp.dot(routed_rows, lax.dynamic_slice_in_dim(w_gate, column_start, HID, 1), preferred_element_type=jnp.float32)
            up_proj = jnp.dot(routed_rows, lax.dynamic_slice_in_dim(w_up, column_start, HID, 1), preferred_element_type=jnp.float32)
            activated = (jax.nn.silu(gate_proj) * up_proj).astype(jnp.bfloat16)
            partial_value = jnp.dot(activated, lax.dynamic_slice_in_dim(w_down, column_start, HID, 0), preferred_element_type=jnp.float32).astype(jnp.bfloat16)
            partial_value = lax.optimization_barrier(partial_value)
            summed = summed + partial_value.astype(jnp.float32)
        for route_rank in range(TOP):
            weight = jnp.where(expert_ids[:, route_rank] == expert, gate_values[:, route_rank], 0.0)
            accumulated = accumulated + weight[:, None] * jnp.take(summed, position[:, route_rank], axis=0)
        return (accumulated, None)
    accumulated, unused = lax.scan(one_expert, jnp.zeros((TOKENS, D), jnp.float32), lax.iota(jnp.int32, EXPERTS))
    return (residual_wide + accumulated).astype(jnp.bfloat16)
```

```python
import jax
import jax.numpy as jnp
from jax import lax
from jax.sharding import PartitionSpec as P

route_scale = 2.5
norm_eps = 1e-06


def flipped(value, distance):
    pairs = [(source, source ^ distance) for source in range(lax.axis_size("expert"))]
    return lax.ppermute(value, "expert", pairs)


def turned(value, shift):
    count = lax.axis_size("groups")
    pairs = [(source, (source + shift) % count) for source in range(count)]
    return lax.ppermute(value, "groups", pairs)


def shards(residual, norm_gain, router, w_gate, w_up, w_down, expert_ids):
    tok_rows, model_width = residual.shape
    top_count = expert_ids.shape[1]
    expert_count = router.shape[1]
    device_count = lax.axis_size("expert")
    groups = lax.axis_size("groups")
    span_size = device_count // expert_count
    capacity = 3 * tok_rows * top_count // (2 * expert_count)
    hidden = w_gate.shape[1]
    part = hidden // groups
    my_group = lax.axis_index("groups")
    lines = [[e * span_size + m for e in range(expert_count)] for m in range(span_size)]

    def cut(start):
        gate_up = jnp.concatenate(
            [
                lax.dynamic_slice_in_dim(w_gate, start, part, 1),
                lax.dynamic_slice_in_dim(w_up, start, part, 1),
            ],
            axis=1,
        )
        return gate_up, lax.dynamic_slice_in_dim(w_down, start, part, 0)

    sent_gate_up, sent_down = cut(my_group * part)
    gate_up_parts = [cut(g * part)[0] for g in range(groups)]
    down_parts = [cut(g * part)[1] for g in range(groups)]

    def span(parts, sent):
        all_parts = list(parts)
        for distance in range(2, span_size, 2):
            first = flipped(sent, distance)
            all_parts += [first] + [turned(first, shift) for shift in range(1, groups)]
        return all_parts + [flipped(p, 1) for p in all_parts]

    gate_up_all = span(gate_up_parts, sent_gate_up)
    down_all = span(down_parts, sent_down)

    residual_wide = residual.astype(jnp.float32)
    mean_square = jnp.mean(residual_wide * residual_wide, axis=1, keepdims=True)
    normed = (residual_wide * lax.rsqrt(mean_square + norm_eps) * norm_gain).astype(jnp.bfloat16)
    picked = expert_ids[:, :, None] == lax.iota(jnp.int32, expert_count)[None, None, :]
    flat_pick = picked.reshape(tok_rows * top_count, expert_count).astype(jnp.int32)
    before = jnp.cumsum(flat_pick, axis=0) - flat_pick
    target = expert_ids.reshape(tok_rows * top_count) * capacity + jnp.sum(
        before * flat_pick, axis=1
    )
    target = target.reshape(tok_rows, top_count)
    places = lax.iota(jnp.int32, expert_count * capacity)
    matches = target[:, :, None] == places[None, None, :]
    assignment = jnp.any(matches, axis=1).astype(jnp.bfloat16)
    packed = lax.dot_general(
        assignment, normed, (((0,), (0,)), ((), ())), preferred_element_type=jnp.float32
    ).astype(jnp.bfloat16)
    rows = lax.all_to_all(
        packed, "expert", split_axis=0, concat_axis=0, axis_index_groups=lines, tiled=True
    )

    logits = jnp.dot(normed, router, preferred_element_type=jnp.float32)
    affinity = jax.nn.sigmoid(logits)
    chosen = jnp.sum(jnp.where(picked, affinity[:, None, :], 0.0), axis=2)
    gate_values = route_scale * chosen / jnp.sum(chosen, axis=1, keepdims=True)

    activated = []
    for gate_up in gate_up_all:
        both = jnp.dot(rows, gate_up, preferred_element_type=jnp.float32)
        activated.append(
            (jax.nn.silu(both[:, :part]) * both[:, part:]).astype(jnp.bfloat16)
        )
    activated = jnp.concatenate(activated, axis=1)
    down = jnp.concatenate(down_all, axis=0)
    expert_out = jnp.dot(activated, down, preferred_element_type=jnp.float32).astype(jnp.bfloat16)
    returned = lax.all_to_all(
        expert_out, "expert", split_axis=0, concat_axis=0, axis_index_groups=lines, tiled=True
    )
    branch = jnp.zeros((tok_rows, model_width), jnp.float32)
    for k in range(top_count):
        found = jnp.dot(
            matches[:, k].astype(jnp.bfloat16), returned, preferred_element_type=jnp.float32
        )
        branch = branch + found * gate_values[:, k : k + 1]
    return (residual_wide + branch).astype(jnp.bfloat16)


def solution(mesh):
    in_specs = (
        P(("groups", "expert"), None),
        P(),
        P(),
        P(None, "expert"),
        P(None, "expert"),
        P("expert", None),
        P(("groups", "expert"), None),
    )
    out_specs = P(("groups", "expert"), None)
    return jax.shard_map(shards, mesh=mesh, in_specs=in_specs, out_specs=out_specs, check_vma=False)
```

```python
import functools

import jax
import jax.numpy as jnp
from jax import lax
from jax.experimental import pallas as pl
from jax.experimental.pallas import tpu as pltpu
from jax.sharding import PartitionSpec as P

route_scale = 2.5
norm_eps = 1e-06
first_share = 2
down_chunks = 2
vmem_bytes = 56 * 1024 * 1024
late_vmem_bytes = 24 * 1024 * 1024


def flipped(value, distance):
    pairs = [(source, source ^ distance) for source in range(lax.axis_size("expert"))]
    return lax.ppermute(value, "expert", pairs)


def turned(value, shift):
    count = lax.axis_size("groups")
    pairs = [(source, (source + shift) % count) for source in range(count)]
    return lax.ppermute(value, "groups", pairs)


def cuts(total, count, unit):
    marks = [total // unit * i // count * unit for i in range(count)] + [total]
    return [(low, high - low) for low, high in zip(marks[:-1], marks[1:])]


def prepare_kernel(block_rows, station, residual, gain, router_t, ids_t, table, packed):
    rows, width = residual.shape
    experts = router_t.shape[0]
    wide = residual[...].astype(jnp.float32)
    mean_square = jnp.mean(wide * wide, axis=1, keepdims=True)
    scale = gain[...].reshape(1, width)
    normed = (wide * lax.rsqrt(mean_square + norm_eps) * scale).astype(jnp.bfloat16)
    here = station[0]
    lane_expert = lax.broadcasted_iota(jnp.int32, (experts, rows), 0) ^ here
    named_t = jnp.zeros((experts, rows), jnp.float32)
    for k in range(ids_t.shape[0]):
        named_t += jnp.where(ids_t[k : k + 1, :] == lane_expert, 1.0, 0.0)
    named_16 = named_t.astype(jnp.bfloat16)
    one = lax.broadcasted_iota(jnp.int32, (rows, rows), 0)
    two = lax.broadcasted_iota(jnp.int32, (rows, rows), 1)
    earlier_t = jnp.where(one < two, 1.0, 0.0).astype(jnp.bfloat16)
    slot_t = jnp.dot(named_16, earlier_t, preferred_element_type=jnp.float32)
    slot_t = jnp.where(named_t > 0.0, slot_t, -1.0)
    place = lax.broadcasted_iota(jnp.int32, (block_rows, rows), 0).astype(jnp.float32)
    for e in range(experts):
        hit = jnp.where(place == slot_t[e : e + 1, :], 1.0, 0.0).astype(jnp.bfloat16)
        block = jnp.dot(hit, normed, preferred_element_type=jnp.float32).astype(jnp.bfloat16)
        start = pl.multiple_of((here ^ e) * block_rows, 16)
        packed[pl.ds(start, block_rows), :] = block
    across = (((1,), (1,)), ((), ()))
    same = jnp.where(one == two, 1.0, 0.0).astype(jnp.bfloat16)
    earlier = jnp.where(two < one, 1.0, 0.0).astype(jnp.bfloat16)
    named = lax.dot_general(same, named_16, across, preferred_element_type=jnp.float32)
    slot = lax.dot_general(earlier, named_16, across, preferred_element_type=jnp.float32)
    slot = jnp.where(named > 0.0, slot, -1.0)
    logits = lax.dot_general(normed, router_t[...], across, preferred_element_type=jnp.float32)
    affinity = jax.nn.sigmoid(logits)
    column = lax.broadcasted_iota(jnp.int32, (rows, experts), 1)
    chosen = []
    for e in range(experts):
        value = jnp.sum(jnp.where(column == (here ^ e), affinity, 0.0), axis=1, keepdims=True)
        chosen.append(jnp.where(named[:, e : e + 1] > 0.0, value, 0.0))
    total = sum(chosen[1:], chosen[0])
    lanes = lax.broadcasted_iota(jnp.int32, (rows, table.shape[1]), 1)
    filled = jnp.zeros((rows, table.shape[1]), jnp.float32)
    for e in range(experts):
        filled = jnp.where(lanes == e, slot[:, e : e + 1], filled)
        filled = jnp.where(lanes == experts + e, route_scale * chosen[e] / total, filled)
    table[pl.ds(0, rows), :] = filled
    table[pl.ds(rows, experts), :] = slot_t


def prepare(residual, norm_gain, router, expert_ids, station, block_rows):
    rows, width = residual.shape
    experts = router.shape[1]
    whole = pl.BlockSpec(memory_space=pltpu.VMEM)
    return pl.pallas_call(
        functools.partial(prepare_kernel, block_rows),
        out_shape=[
            jax.ShapeDtypeStruct((rows + experts, rows), jnp.float32),
            jax.ShapeDtypeStruct((experts * block_rows, width), jnp.bfloat16),
        ],
        in_specs=[pl.BlockSpec(memory_space=pltpu.SMEM)] + [whole] * 4,
        out_specs=[whole] * 2,
        compiler_params=pltpu.CompilerParams(vmem_limit_bytes=vmem_bytes),
    )(station[None], residual, norm_gain, router.T, expert_ids.T)


def moved(copies, sems):
    return [pltpu.make_async_copy(a, b, sems.at[i]) for i, (a, b) in enumerate(copies)]


def down_pieces(refs, target, copies, group, hidden, groups):
    pieces = []
    for ref, (member, shift, rows, column, columns) in zip(refs, copies):
        start = member * hidden
        if shift is not None:
            part = lax.rem(group + groups - shift, groups)
            start = pl.multiple_of(part * (hidden // groups) + start, 16)
        pieces.append((ref.at[:, pl.ds(column, columns)], target.at[pl.ds(start, rows), :]))
    return pieces


def down_product(act, wd, outs):
    block_rows = outs[0].shape[0]
    width = wd.shape[1]
    step = 256 if width % 256 == 0 else 128
    for base in range(0, width, step):
        span = pl.ds(base, step)
        value = jnp.dot(act[...], wd[:, span], preferred_element_type=jnp.float32)
        value = value.astype(jnp.bfloat16)
        for i, out in enumerate(outs):
            out[:, span] = value[i * block_rows : (i + 1) * block_rows, :]


def expert_kernel(plan, group, station, rows, *refs):
    block_rows, hidden, width, groups, weight_copies, down_copies = plan
    weight_refs, refs = refs[: len(weight_copies)], refs[len(weight_copies) :]
    down_refs, refs = refs[: len(down_copies)], refs[len(down_copies) :]
    act, outs, (x, w, wd, row_sems, weight_sems, down_sems) = refs[0], refs[1:-6], refs[-6:]
    members = w.shape[0]
    g = group[0]
    row_pieces = []
    for r in range(x.shape[0] // block_rows):
        start = pl.multiple_of((station[0] ^ r) * block_rows, 16)
        row_pieces.append(
            (rows.at[pl.ds(start, block_rows), :], x.at[pl.ds(r * block_rows, block_rows), :])
        )
    row_waits = moved(row_pieces, row_sems)
    stages = [[] for _ in range(members)]
    pieces = []
    for ref, (member, shift, base, size, column) in zip(weight_refs, weight_copies):
        start = base
        if shift is not None:
            part = lax.rem(g + groups - shift, groups)
            start = pl.multiple_of(part * (width // groups) + base, 16)
        pieces.append((ref, w.at[member, pl.ds(start, size), pl.ds(column, hidden)]))
    for copy, (member, *_) in zip(moved(pieces, weight_sems), weight_copies):
        stages[member].append(copy)
    stages.append(moved(down_pieces(down_refs, wd, down_copies, g, hidden, groups), down_sems))

    for copy in row_waits + stages[0]:
        copy.start()
    for copy in row_waits:
        copy.wait()
    for copy in stages[1]:
        copy.start()
    for member in range(members):
        for copy in stages[member]:
            copy.wait()
        if member + 2 <= members:
            for copy in stages[member + 2]:
                copy.start()
        gate = jnp.dot(x[...], w[member, :, :hidden], preferred_element_type=jnp.float32)
        up = jnp.dot(x[...], w[member, :, hidden:], preferred_element_type=jnp.float32)
        act[:, member * hidden : (member + 1) * hidden] = (
            gate / (1.0 + jnp.exp(-gate)) * up
        ).astype(jnp.bfloat16)
    for copy in stages[members]:
        copy.wait()
    down_product(act, wd, outs)


def expert_first(group, station, rows, weights, copies, downs, down_copies, sizes, members):
    block_rows, hidden, groups = sizes
    total_rows, width = rows.shape
    columns = down_copies[0][-1]
    blocks = total_rows // block_rows
    plan = (block_rows, hidden, width, groups, copies, down_copies)
    out = pl.pallas_call(
        functools.partial(expert_kernel, plan),
        out_shape=[jax.ShapeDtypeStruct((total_rows, members * hidden), jnp.bfloat16)]
        + [jax.ShapeDtypeStruct((block_rows, columns), jnp.bfloat16)] * blocks,
        in_specs=[pl.BlockSpec(memory_space=pltpu.SMEM)] * 2
        + [pl.BlockSpec(memory_space=pl.ANY)] * (1 + len(copies) + len(down_copies)),
        out_specs=[pl.BlockSpec(memory_space=pltpu.VMEM)] * (1 + blocks),
        scratch_shapes=[
            pltpu.VMEM((total_rows, width), jnp.bfloat16),
            pltpu.VMEM((members, width, 2 * hidden), jnp.bfloat16),
            pltpu.VMEM((members * hidden, columns), jnp.bfloat16),
            pltpu.SemaphoreType.DMA((blocks,)),
            pltpu.SemaphoreType.DMA((len(copies),)),
            pltpu.SemaphoreType.DMA((len(down_copies),)),
        ],
        compiler_params=pltpu.CompilerParams(vmem_limit_bytes=vmem_bytes),
    )(group, station, rows, *weights, *downs)
    return out[0], out[1:]


def down_kernel(plan, group, act, *refs):
    hidden, groups, copies = plan
    down_refs, outs, (wd, sems) = refs[: len(copies)], refs[len(copies) : -2], refs[-2:]
    waits = moved(down_pieces(down_refs, wd, copies, group[0], hidden, groups), sems)
    for copy in waits:
        copy.start()
    for copy in waits:
        copy.wait()
    down_product(act, wd, outs)


def expert_later(group, act, downs, copies, sizes):
    block_rows, hidden, groups = sizes
    blocks = act.shape[0] // block_rows
    columns = copies[0][-1]
    whole = pl.BlockSpec(memory_space=pltpu.VMEM)
    return pl.pallas_call(
        functools.partial(down_kernel, (hidden, groups, copies)),
        out_shape=[jax.ShapeDtypeStruct((block_rows, columns), jnp.bfloat16)] * blocks,
        in_specs=[pl.BlockSpec(memory_space=pltpu.SMEM), whole]
        + [pl.BlockSpec(memory_space=pl.ANY)] * len(downs),
        out_specs=[whole] * blocks,
        scratch_shapes=[
            pltpu.VMEM((act.shape[1], columns), jnp.bfloat16),
            pltpu.SemaphoreType.DMA((len(copies),)),
        ],
        compiler_params=pltpu.CompilerParams(vmem_limit_bytes=late_vmem_bytes),
    )(group, act, *downs)


def weighted_sum(classes, is_hub, table, blocks, high, low):
    block_rows = blocks[0].shape[0]
    rows = table.shape[1]
    experts = table.shape[0] - rows
    place = lax.broadcasted_iota(jnp.int32, (rows, block_rows), 1).astype(jnp.float32)
    for i, (e, at_hub) in enumerate(classes):
        gate = table[pl.ds(0, rows), experts + e : experts + e + 1]
        if not at_hub:
            gate = jnp.where(is_hub[0] == 1, 0.0, gate)
        weight = jnp.where(place == table[pl.ds(0, rows), e : e + 1], gate, 0.0)
        upper = weight.astype(jnp.bfloat16)
        columns = pl.ds(i * block_rows, block_rows)
        high[:, columns] = upper
        low[:, columns] = (weight - upper.astype(jnp.float32)).astype(jnp.bfloat16)
    stacked = jnp.concatenate([block[...] for block in blocks], axis=0)
    total = jnp.dot(high[...], stacked, preferred_element_type=jnp.float32)
    return total + jnp.dot(low[...], stacked, preferred_element_type=jnp.float32)


def partner_kernel(classes, is_hub, table, *refs):
    blocks, (out, high, low) = refs[:-3], refs[-3:]
    out[...] = weighted_sum(classes, is_hub, table, blocks, high, low).astype(jnp.bfloat16)


def partner_sum(classes, is_hub, table, blocks):
    block_rows, width = blocks[0].shape
    rows = table.shape[1]
    whole = pl.BlockSpec(memory_space=pltpu.VMEM)
    return pl.pallas_call(
        functools.partial(partner_kernel, classes),
        out_shape=jax.ShapeDtypeStruct((rows, width), jnp.bfloat16),
        in_specs=[pl.BlockSpec(memory_space=pltpu.SMEM)] + [whole] * (1 + len(blocks)),
        out_specs=whole,
        scratch_shapes=[pltpu.VMEM((rows, block_rows * len(blocks)), jnp.bfloat16)] * 2,
        compiler_params=pltpu.CompilerParams(vmem_limit_bytes=late_vmem_bytes),
    )(is_hub, table, *blocks)


def result_kernel(plan, is_hub, table, *refs):
    classes, base, size, first = plan
    count = len(classes)
    blocks = refs[:count]
    hub_sum, residual = refs[count : count + 2]
    out, high, low, held, result, sems = refs[-6:]
    span = pl.ds(base, size)
    fetch = pltpu.make_async_copy(residual.at[:, span], held, sems.at[0])
    fetch.start()
    total = weighted_sum(classes, is_hub, table, blocks, high, low)
    fetch.wait()
    total += held[...].astype(jnp.float32) + hub_sum[...].astype(jnp.float32)
    result[...] = total.astype(jnp.bfloat16)
    store = pltpu.make_async_copy(result, out.at[:, span], sems.at[1])
    store.start()
    store.wait()


def result(classes, is_hub, table, blocks, hub_sum, residual, base, size, so_far):
    block_rows = blocks[0].shape[0]
    rows, width = residual.shape
    whole = pl.BlockSpec(memory_space=pltpu.VMEM)
    anywhere = pl.BlockSpec(memory_space=pl.ANY)
    first = so_far is None
    earlier = [] if first else [so_far]
    return pl.pallas_call(
        functools.partial(result_kernel, (classes, base, size, first)),
        out_shape=jax.ShapeDtypeStruct((rows, width), jnp.bfloat16),
        in_specs=[pl.BlockSpec(memory_space=pltpu.SMEM)]
        + [whole] * (2 + len(blocks))
        + [anywhere] * (1 + len(earlier)),
        out_specs=anywhere,
        scratch_shapes=[pltpu.VMEM((rows, block_rows * len(blocks)), jnp.bfloat16)] * 2
        + [pltpu.VMEM((rows, size), jnp.bfloat16)] * 2
        + [pltpu.SemaphoreType.DMA((2,))],
        input_output_aliases={} if first else {len(blocks) + 4: 0},
        compiler_params=pltpu.CompilerParams(vmem_limit_bytes=late_vmem_bytes),
    )(is_hub, table, *blocks, hub_sum, residual, *earlier)


def named(name, function, *args):
    with jax.named_scope(name):
        return function(*args)


def after(value, *others):
    return lax.optimization_barrier((value,) + others)[0]


def shards(residual, norm_gain, router, w_gate, w_up, w_down, expert_ids):
    tok_rows, width = residual.shape
    top = expert_ids.shape[1]
    experts = router.shape[1]
    device_count = lax.axis_size("expert")
    groups = lax.axis_size("groups")
    members = device_count // experts
    hidden = w_gate.shape[1]
    capacity = 3 * tok_rows * top // (2 * experts)
    block_rows = -(-capacity // 16) * 16
    my_group = lax.axis_index("groups")
    station = (lax.axis_index("expert") // members).astype(jnp.int32)
    half = experts // 2
    last = experts - 1
    hubs = (half - 1, half)
    is_hub = jnp.logical_or(station == hubs[0], station == hubs[1]).astype(jnp.int32)[None]

    def along(value, route):
        pairs = [
            (a * members + m, b * members + m) for a, b in route.items() for m in range(members)
        ]
        return lax.ppermute(value, "expert", pairs)

    near = {r: {z: z ^ r for z in range(experts)} for r in range(1, half)}
    mixed = {
        r: {z: z ^ (r ^ last if z in hubs else r) for z in range(experts)}
        for r in range(half, last)
    }
    far = {z: z ^ last for z in range(experts) if z not in hubs}
    between = {hubs[0]: hubs[1], hubs[1]: hubs[0]}

    part_width, part_hidden = width // groups, hidden // groups
    jobs = []
    for distance in range(2, members, 2):
        for i, w in enumerate((w_gate, w_up)):
            early = part_width // ((first_share if i == 0 else 2) * 16) * 16
            for base, size in ((0, early), (early, part_width - early)):
                sent = lax.dynamic_slice_in_dim(w, my_group * part_width + base, size, 0)
                jobs.append((sent, distance, (base, size, i * hidden), None))
    columns = cuts(width, down_chunks, 128)
    for c, (base, size) in enumerate(columns):
        for distance in range(2, members, 2):
            sent = lax.dynamic_slice(w_down, (my_group * part_hidden, base), (part_hidden, size))
            jobs.append((sent, distance, None, c))
    table, packed = prepare(after(residual, jobs[0][0]), norm_gain, router, expert_ids, station, block_rows)
    lines = [[e * members + m for e in range(experts)] for m in range(members)]
    hub_table = named("table", along, table, between)

    last_job = len(jobs) - 1
    group = my_group[None].astype(jnp.int32)
    weights = [w_gate, w_up] + [named("own", flipped, w, 1) for w in (w_gate, w_up)]
    copies = [(m, None, 0, width, i * hidden) for m in range(2) for i in range(2)]
    own_down = named("own", flipped, w_down, 1)
    downs = [[w_down, own_down] for _ in columns]
    down_copies = [[(m, None, hidden, base, size) for m in range(2)] for base, size in columns]
    Y, X = [], []
    rows = None
    for n, (sent, distance, gate_up, chunk) in enumerate(jobs):
        Y.append(named(f"Y{n}", flipped, after(sent, *Y[-1:], *(X[-2] if n > 1 else [])), distance))
        if n == 0:
            packed = after(packed, Y[0], hub_table)
            rows = lax.all_to_all(packed, "expert", 0, 0, axis_index_groups=lines, tiled=True)
        ready = after(Y[n], *X[-1]) if X else Y[n]
        X.append([named(f"X{n}", turned, ready, shift) for shift in range(1, groups)])
    sizes = (block_rows, hidden, groups)
    first_jobs = sum(1 for job in jobs if job[3] in (None, 0))
    act = None
    for n, (sent, distance, gate_up, chunk) in enumerate(jobs):
        if n == first_jobs:
            act, first_outs = expert_first(
                group, station[None], rows, weights, copies, downs[0], down_copies[0], sizes, members
            )
        for offset in range(2):
            for shift, part in enumerate([Y[n]] + X[n]):
                if offset:
                    part = named(f"C{n}", flipped, part if act is None else after(part, act), 1)
                if gate_up is not None:
                    base, size, column = gate_up
                    weights.append(part)
                    copies.append((distance + offset, shift, base, size, column))
                else:
                    downs[chunk].append(part)
                    down_copies[chunk].append(
                        (distance + offset, shift, part_hidden, 0, columns[chunk][1])
                    )

    partner = [(r, True) for r in mixed] + [(last, True)]
    classes = [(r, r < half) for r in range(experts)]
    layer_out = None
    for c, (base, size) in enumerate(columns):
        outs = first_outs if c == 0 else expert_later(group, act, downs[c], down_copies[c], sizes)
        back = [outs[0]] + [None] * last
        for r in mixed:
            route = {b: a for a, b in mixed[r].items()}
            back[r] = named(f"mixed_back{c}", along, outs[r], route)
        back[last] = named(f"far_back{c}", along, outs[last], far)
        for r in near:
            back[r] = named(f"near_back{c}", along, outs[r], near[r])
        held = [back[r] for r in mixed] + [outs[last]]
        hub_sum = partner_sum(partner, is_hub, hub_table, held)
        hub_sum = named(f"sum_back{c}", along, hub_sum, between)
        layer_out = result(
            classes, is_hub, table, back, hub_sum, residual, base, size, layer_out
        )
    return layer_out


def solution(mesh):
    in_specs = (
        P(("groups", "expert"), None),
        P(),
        P(),
        P(None, "expert"),
        P(None, "expert"),
        P("expert", None),
        P(("groups", "expert"), None),
    )
    out_specs = P(("groups", "expert"), None)
    return jax.shard_map(shards, mesh=mesh, in_specs=in_specs, out_specs=out_specs, check_vma=False)
```

```python
import functools

import jax
import jax.numpy as jnp
from jax import lax
from jax.experimental import pallas as pl
from jax.experimental.pallas import tpu as pltpu
from jax.sharding import PartitionSpec as P

route_scale = 2.5
norm_eps = 1e-06
first_share = 2
down_chunks = 2
vmem_bytes = 56 * 1024 * 1024
late_vmem_bytes = 24 * 1024 * 1024


def flipped(value, distance):
    pairs = [(source, source ^ distance) for source in range(lax.axis_size("expert"))]
    return lax.ppermute(value, "expert", pairs)


def turned(value, shift):
    count = lax.axis_size("groups")
    pairs = [(source, (source + shift) % count) for source in range(count)]
    return lax.ppermute(value, "groups", pairs)


def cuts(total, count, unit):
    marks = [total // unit * i // count * unit for i in range(count)] + [total]
    return [(low, high - low) for low, high in zip(marks[:-1], marks[1:])]


def prepare_kernel(block_rows, station, residual, gain, router_t, ids_t, table, packed):
    rows, width = residual.shape
    experts = router_t.shape[0]
    wide = residual[...].astype(jnp.float32)
    mean_square = jnp.mean(wide * wide, axis=1, keepdims=True)
    scale = gain[...].reshape(1, width)
    normed = (wide * lax.rsqrt(mean_square + norm_eps) * scale).astype(jnp.bfloat16)
    here = station[0]
    lane_expert = lax.broadcasted_iota(jnp.int32, (experts, rows), 0) ^ here
    named_t = jnp.zeros((experts, rows), jnp.float32)
    for k in range(ids_t.shape[0]):
        named_t += jnp.where(ids_t[k : k + 1, :] == lane_expert, 1.0, 0.0)
    named_16 = named_t.astype(jnp.bfloat16)
    one = lax.broadcasted_iota(jnp.int32, (rows, rows), 0)
    two = lax.broadcasted_iota(jnp.int32, (rows, rows), 1)
    earlier_t = jnp.where(one < two, 1.0, 0.0).astype(jnp.bfloat16)
    slot_t = jnp.dot(named_16, earlier_t, preferred_element_type=jnp.float32)
    slot_t = jnp.where(named_t > 0.0, slot_t, -1.0)
    place = lax.broadcasted_iota(jnp.int32, (block_rows, rows), 0).astype(jnp.float32)
    for e in range(experts):
        hit = jnp.where(place == slot_t[e : e + 1, :], 1.0, 0.0).astype(jnp.bfloat16)
        block = jnp.dot(hit, normed, preferred_element_type=jnp.float32).astype(jnp.bfloat16)
        start = pl.multiple_of((here ^ e) * block_rows, 16)
        packed[pl.ds(start, block_rows), :] = block
    across = (((1,), (1,)), ((), ()))
    same = jnp.where(one == two, 1.0, 0.0).astype(jnp.bfloat16)
    earlier = jnp.where(two < one, 1.0, 0.0).astype(jnp.bfloat16)
    named = lax.dot_general(same, named_16, across, preferred_element_type=jnp.float32)
    slot = lax.dot_general(earlier, named_16, across, preferred_element_type=jnp.float32)
    slot = jnp.where(named > 0.0, slot, -1.0)
    logits = lax.dot_general(normed, router_t[...], across, preferred_element_type=jnp.float32)
    affinity = jax.nn.sigmoid(logits)
    column = lax.broadcasted_iota(jnp.int32, (rows, experts), 1)
    chosen = []
    for e in range(experts):
        value = jnp.sum(jnp.where(column == (here ^ e), affinity, 0.0), axis=1, keepdims=True)
        chosen.append(jnp.where(named[:, e : e + 1] > 0.0, value, 0.0))
    total = sum(chosen[1:], chosen[0])
    lanes = lax.broadcasted_iota(jnp.int32, (rows, table.shape[1]), 1)
    filled = jnp.zeros((rows, table.shape[1]), jnp.float32)
    for e in range(experts):
        filled = jnp.where(lanes == e, slot[:, e : e + 1], filled)
        filled = jnp.where(lanes == experts + e, route_scale * chosen[e] / total, filled)
    table[...] = filled


def prepare(residual, norm_gain, router, expert_ids, station, block_rows):
    rows, width = residual.shape
    experts = router.shape[1]
    whole = pl.BlockSpec(memory_space=pltpu.VMEM)
    return pl.pallas_call(
        functools.partial(prepare_kernel, block_rows),
        out_shape=[
            jax.ShapeDtypeStruct((rows, 128), jnp.float32),
            jax.ShapeDtypeStruct((experts * block_rows, width), jnp.bfloat16),
        ],
        in_specs=[pl.BlockSpec(memory_space=pltpu.SMEM)] + [whole] * 4,
        out_specs=[whole] * 2,
        compiler_params=pltpu.CompilerParams(vmem_limit_bytes=vmem_bytes),
    )(station[None], residual, norm_gain, router.T, expert_ids.T)


def moved(copies, sems):
    return [pltpu.make_async_copy(a, b, sems.at[i]) for i, (a, b) in enumerate(copies)]


def down_pieces(refs, target, copies, group, hidden, groups):
    pieces = []
    for ref, (member, shift, rows, column, columns) in zip(refs, copies):
        start = member * hidden
        if shift is not None:
            part = lax.rem(group + groups - shift, groups)
            start = pl.multiple_of(part * (hidden // groups) + start, 16)
        pieces.append((ref.at[:, pl.ds(column, columns)], target.at[pl.ds(start, rows), :]))
    return pieces


def down_product(act, wd, outs):
    block_rows = outs[0].shape[0]
    width = wd.shape[1]
    step = 256 if width % 256 == 0 else 128
    for base in range(0, width, step):
        span = pl.ds(base, step)
        value = jnp.dot(act[...], wd[:, span], preferred_element_type=jnp.float32)
        value = value.astype(jnp.bfloat16)
        for i, out in enumerate(outs):
            out[:, span] = value[i * block_rows : (i + 1) * block_rows, :]


def expert_kernel(plan, group, station, rows, *refs):
    block_rows, hidden, width, groups, weight_copies, down_copies = plan
    weight_refs, refs = refs[: len(weight_copies)], refs[len(weight_copies) :]
    down_refs, refs = refs[: len(down_copies)], refs[len(down_copies) :]
    act, outs, (x, w, wd, row_sems, weight_sems, down_sems) = refs[0], refs[1:-6], refs[-6:]
    members = w.shape[0]
    g = group[0]
    row_pieces = []
    for r in range(x.shape[0] // block_rows):
        start = pl.multiple_of((station[0] ^ r) * block_rows, 16)
        row_pieces.append(
            (rows.at[pl.ds(start, block_rows), :], x.at[pl.ds(r * block_rows, block_rows), :])
        )
    row_waits = moved(row_pieces, row_sems)
    stages = [[] for _ in range(members)]
    pieces = []
    for ref, (member, shift, base, size, column) in zip(weight_refs, weight_copies):
        start = base
        if shift is not None:
            part = lax.rem(g + groups - shift, groups)
            start = pl.multiple_of(part * (width // groups) + base, 16)
        pieces.append((ref, w.at[member, pl.ds(start, size), pl.ds(column, hidden)]))
    for copy, (member, *_) in zip(moved(pieces, weight_sems), weight_copies):
        stages[member].append(copy)
    stages.append(moved(down_pieces(down_refs, wd, down_copies, g, hidden, groups), down_sems))

    for copy in row_waits + stages[0]:
        copy.start()
    for copy in row_waits:
        copy.wait()
    for copy in stages[1]:
        copy.start()
    for member in range(members):
        for copy in stages[member]:
            copy.wait()
        if member + 2 <= members:
            for copy in stages[member + 2]:
                copy.start()
        gate = jnp.dot(x[...], w[member, :, :hidden], preferred_element_type=jnp.float32)
        up = jnp.dot(x[...], w[member, :, hidden:], preferred_element_type=jnp.float32)
        act[:, member * hidden : (member + 1) * hidden] = (
            gate / (1.0 + jnp.exp(-gate)) * up
        ).astype(jnp.bfloat16)
    for copy in stages[members]:
        copy.wait()
    down_product(act, wd, outs)


def expert_first(group, station, rows, weights, copies, downs, down_copies, sizes, members):
    block_rows, hidden, groups = sizes
    total_rows, width = rows.shape
    columns = down_copies[0][-1]
    blocks = total_rows // block_rows
    plan = (block_rows, hidden, width, groups, copies, down_copies)
    out = pl.pallas_call(
        functools.partial(expert_kernel, plan),
        out_shape=[jax.ShapeDtypeStruct((total_rows, members * hidden), jnp.bfloat16)]
        + [jax.ShapeDtypeStruct((block_rows, columns), jnp.bfloat16)] * blocks,
        in_specs=[pl.BlockSpec(memory_space=pltpu.SMEM)] * 2
        + [pl.BlockSpec(memory_space=pl.ANY)] * (1 + len(copies) + len(down_copies)),
        out_specs=[pl.BlockSpec(memory_space=pltpu.VMEM)] * (1 + blocks),
        scratch_shapes=[
            pltpu.VMEM((total_rows, width), jnp.bfloat16),
            pltpu.VMEM((members, width, 2 * hidden), jnp.bfloat16),
            pltpu.VMEM((members * hidden, columns), jnp.bfloat16),
            pltpu.SemaphoreType.DMA((blocks,)),
            pltpu.SemaphoreType.DMA((len(copies),)),
            pltpu.SemaphoreType.DMA((len(down_copies),)),
        ],
        compiler_params=pltpu.CompilerParams(vmem_limit_bytes=vmem_bytes),
    )(group, station, rows, *weights, *downs)
    return out[0], out[1:]


def down_kernel(plan, group, act, *refs):
    hidden, groups, copies = plan
    down_refs, outs, (wd, sems) = refs[: len(copies)], refs[len(copies) : -2], refs[-2:]
    waits = moved(down_pieces(down_refs, wd, copies, group[0], hidden, groups), sems)
    for copy in waits:
        copy.start()
    for copy in waits:
        copy.wait()
    down_product(act, wd, outs)


def expert_later(group, act, downs, copies, sizes):
    block_rows, hidden, groups = sizes
    blocks = act.shape[0] // block_rows
    columns = copies[0][-1]
    whole = pl.BlockSpec(memory_space=pltpu.VMEM)
    return pl.pallas_call(
        functools.partial(down_kernel, (hidden, groups, copies)),
        out_shape=[jax.ShapeDtypeStruct((block_rows, columns), jnp.bfloat16)] * blocks,
        in_specs=[pl.BlockSpec(memory_space=pltpu.SMEM), whole]
        + [pl.BlockSpec(memory_space=pl.ANY)] * len(downs),
        out_specs=[whole] * blocks,
        scratch_shapes=[
            pltpu.VMEM((act.shape[1], columns), jnp.bfloat16),
            pltpu.SemaphoreType.DMA((len(copies),)),
        ],
        compiler_params=pltpu.CompilerParams(vmem_limit_bytes=late_vmem_bytes),
    )(group, act, *downs)


def lanes_for(count):
    return -(-count // 128) * 128


def weighted_sum(plan, is_hub, table, blocks, high, low):
    classes, experts = plan
    block_rows = blocks[0].shape[0]
    rows = table.shape[0]
    used = pl.ds(0, block_rows * len(blocks))
    place = lax.broadcasted_iota(jnp.int32, (rows, block_rows), 1).astype(jnp.float32)
    for i, (e, at_hub) in enumerate(classes):
        gate = table[:, experts + e : experts + e + 1]
        if not at_hub:
            gate = jnp.where(is_hub[0] == 1, 0.0, gate)
        weight = jnp.where(place == table[:, e : e + 1], gate, 0.0)
        upper = weight.astype(jnp.bfloat16)
        columns = pl.ds(i * block_rows, block_rows)
        high[:, columns] = upper
        low[:, columns] = (weight - upper.astype(jnp.float32)).astype(jnp.bfloat16)
    stacked = jnp.concatenate([block[...] for block in blocks], axis=0)
    total = jnp.dot(high[:, used], stacked, preferred_element_type=jnp.float32)
    return total + jnp.dot(low[:, used], stacked, preferred_element_type=jnp.float32)


def partner_kernel(plan, is_hub, table, *refs):
    blocks, (out, high, low) = refs[:-3], refs[-3:]
    out[...] = weighted_sum(plan, is_hub, table, blocks, high, low).astype(jnp.bfloat16)


def partner_sum(plan, is_hub, table, blocks):
    block_rows, width = blocks[0].shape
    rows = table.shape[0]
    whole = pl.BlockSpec(memory_space=pltpu.VMEM)
    return pl.pallas_call(
        functools.partial(partner_kernel, plan),
        out_shape=jax.ShapeDtypeStruct((rows, width), jnp.bfloat16),
        in_specs=[pl.BlockSpec(memory_space=pltpu.SMEM)] + [whole] * (1 + len(blocks)),
        out_specs=whole,
        scratch_shapes=[pltpu.VMEM((rows, lanes_for(block_rows * len(blocks))), jnp.bfloat16)] * 2,
        compiler_params=pltpu.CompilerParams(vmem_limit_bytes=late_vmem_bytes),
    )(is_hub, table, *blocks)


def result_kernel(plan, is_hub, table, *refs):
    sum_plan, base, size = plan
    count = len(sum_plan[0])
    blocks = refs[:count]
    hub_sum, residual = refs[count : count + 2]
    out, high, low, held, result, sems = refs[-6:]
    span = pl.ds(base, size)
    fetch = pltpu.make_async_copy(residual.at[:, span], held, sems.at[0])
    fetch.start()
    total = weighted_sum(sum_plan, is_hub, table, blocks, high, low)
    fetch.wait()
    total += held[...].astype(jnp.float32) + hub_sum[...].astype(jnp.float32)
    result[...] = total.astype(jnp.bfloat16)
    store = pltpu.make_async_copy(result, out.at[:, span], sems.at[1])
    store.start()
    store.wait()


def result(plan, is_hub, table, blocks, hub_sum, residual, base, size, so_far):
    block_rows = blocks[0].shape[0]
    rows, width = residual.shape
    whole = pl.BlockSpec(memory_space=pltpu.VMEM)
    anywhere = pl.BlockSpec(memory_space=pl.ANY)
    first = so_far is None
    earlier = [] if first else [so_far]
    return pl.pallas_call(
        functools.partial(result_kernel, (plan, base, size)),
        out_shape=jax.ShapeDtypeStruct((rows, width), jnp.bfloat16),
        in_specs=[pl.BlockSpec(memory_space=pltpu.SMEM)]
        + [whole] * (2 + len(blocks))
        + [anywhere] * (1 + len(earlier)),
        out_specs=anywhere,
        scratch_shapes=[pltpu.VMEM((rows, lanes_for(block_rows * len(blocks))), jnp.bfloat16)] * 2
        + [pltpu.VMEM((rows, size), jnp.bfloat16)] * 2
        + [pltpu.SemaphoreType.DMA((2,))],
        input_output_aliases={} if first else {len(blocks) + 4: 0},
        compiler_params=pltpu.CompilerParams(vmem_limit_bytes=late_vmem_bytes),
    )(is_hub, table, *blocks, hub_sum, residual, *earlier)


def named(name, function, *args):
    with jax.named_scope(name):
        return function(*args)


def after(value, *others):
    return lax.optimization_barrier((value,) + others)[0]


def shards(residual, norm_gain, router, w_gate, w_up, w_down, expert_ids):
    tok_rows, width = residual.shape
    top = expert_ids.shape[1]
    experts = router.shape[1]
    device_count = lax.axis_size("expert")
    groups = lax.axis_size("groups")
    members = device_count // experts
    hidden = w_gate.shape[1]
    capacity = 3 * tok_rows * top // (2 * experts)
    block_rows = -(-capacity // 16) * 16
    my_group = lax.axis_index("groups")
    station = (lax.axis_index("expert") // members).astype(jnp.int32)
    half = experts // 2
    last = experts - 1
    hubs = (half - 1, half)
    is_hub = jnp.logical_or(station == hubs[0], station == hubs[1]).astype(jnp.int32)[None]

    def along(value, route):
        pairs = [
            (a * members + m, b * members + m) for a, b in route.items() for m in range(members)
        ]
        return lax.ppermute(value, "expert", pairs)

    near = {r: {z: z ^ r for z in range(experts)} for r in range(1, half)}
    mixed = {
        r: {z: z ^ (r ^ last if z in hubs else r) for z in range(experts)}
        for r in range(half, last)
    }
    far = {z: z ^ last for z in range(experts) if z not in hubs}
    between = {hubs[0]: hubs[1], hubs[1]: hubs[0]}

    part_width, part_hidden = width // groups, hidden // groups
    jobs = []
    for distance in range(2, members, 2):
        for i, w in enumerate((w_gate, w_up)):
            early = part_width // ((first_share if i == 0 else 2) * 16) * 16
            for base, size in ((0, early), (early, part_width - early)):
                sent = lax.dynamic_slice_in_dim(w, my_group * part_width + base, size, 0)
                jobs.append((sent, distance, (base, size, i * hidden), None))
    columns = cuts(width, down_chunks, 128)
    for c, (base, size) in enumerate(columns):
        for distance in range(2, members, 2):
            sent = lax.dynamic_slice(w_down, (my_group * part_hidden, base), (part_hidden, size))
            jobs.append((sent, distance, None, c))
    table, packed = prepare(after(residual, jobs[0][0]), norm_gain, router, expert_ids, station, block_rows)
    lines = [[e * members + m for e in range(experts)] for m in range(members)]
    hub_table = named("table", along, table, between)

    last_job = len(jobs) - 1
    group = my_group[None].astype(jnp.int32)
    weights = [w_gate, w_up] + [named("own", flipped, w, 1) for w in (w_gate, w_up)]
    copies = [(m, None, 0, width, i * hidden) for m in range(2) for i in range(2)]
    own_down = named("own", flipped, w_down, 1)
    downs = [[w_down, own_down] for _ in columns]
    down_copies = [[(m, None, hidden, base, size) for m in range(2)] for base, size in columns]
    Y, X = [], []
    rows = None
    for n, (sent, distance, gate_up, chunk) in enumerate(jobs):
        Y.append(named(f"Y{n}", flipped, after(sent, *Y[-1:], *(X[-2] if n > 1 else [])), distance))
        if n == 0:
            packed = after(packed, Y[0], hub_table)
            rows = lax.all_to_all(packed, "expert", 0, 0, axis_index_groups=lines, tiled=True)
        ready = after(Y[n], *X[-1]) if X else Y[n]
        X.append([named(f"X{n}", turned, ready, shift) for shift in range(1, groups)])
    sizes = (block_rows, hidden, groups)
    first_jobs = sum(1 for job in jobs if job[3] in (None, 0))
    act = None
    for n, (sent, distance, gate_up, chunk) in enumerate(jobs):
        if n == first_jobs:
            act, first_outs = expert_first(
                group, station[None], rows, weights, copies, downs[0], down_copies[0], sizes, members
            )
        for offset in range(2):
            for shift, part in enumerate([Y[n]] + X[n]):
                if offset:
                    part = named(f"C{n}", flipped, part if act is None else after(part, act), 1)
                if gate_up is not None:
                    base, size, column = gate_up
                    weights.append(part)
                    copies.append((distance + offset, shift, base, size, column))
                else:
                    downs[chunk].append(part)
                    down_copies[chunk].append(
                        (distance + offset, shift, part_hidden, 0, columns[chunk][1])
                    )

    partner = [(r, True) for r in mixed] + [(last, True)]
    classes = [(r, r < half) for r in range(experts)]
    layer_out = None
    for c, (base, size) in enumerate(columns):
        outs = first_outs if c == 0 else expert_later(group, act, downs[c], down_copies[c], sizes)
        back = [outs[0]] + [None] * last
        for r in mixed:
            route = {b: a for a, b in mixed[r].items()}
            back[r] = named(f"mixed_back{c}", along, outs[r], route)
        back[last] = named(f"far_back{c}", along, outs[last], far)
        for r in near:
            back[r] = named(f"near_back{c}", along, outs[r], near[r])
        held = [back[r] for r in mixed] + [outs[last]]
        hub_sum = partner_sum((partner, experts), is_hub, hub_table, held)
        hub_sum = named(f"sum_back{c}", along, hub_sum, between)
        layer_out = result(
            (classes, experts), is_hub, table, back, hub_sum, residual, base, size, layer_out
        )
    return layer_out


def solution(mesh):
    in_specs = (
        P(("groups", "expert"), None),
        P(),
        P(),
        P(None, "expert"),
        P(None, "expert"),
        P("expert", None),
        P(("groups", "expert"), None),
    )
    out_specs = P(("groups", "expert"), None)
    return jax.shard_map(shards, mesh=mesh, in_specs=in_specs, out_specs=out_specs, check_vma=False)
```

```python
import functools

import jax
import jax.numpy as jnp
from jax import lax
from jax.experimental import pallas as pl
from jax.experimental.pallas import tpu as pltpu
from jax.sharding import PartitionSpec as P

route_scale = 2.5
norm_eps = 1e-06
first_share = 2
down_chunks = 2
vmem_bytes = 56 * 1024 * 1024
late_vmem_bytes = 24 * 1024 * 1024


def flipped(value, distance):
    pairs = [(source, source ^ distance) for source in range(lax.axis_size("expert"))]
    return lax.ppermute(value, "expert", pairs)


def turned(value, shift):
    count = lax.axis_size("groups")
    pairs = [(source, (source + shift) % count) for source in range(count)]
    return lax.ppermute(value, "groups", pairs)


def cuts(total, count, unit):
    marks = [total // unit * i // count * unit for i in range(count)] + [total]
    return [(low, high - low) for low, high in zip(marks[:-1], marks[1:])]


def prepare_kernel(block_rows, station, residual, gain, router_t, ids_t, table, packed):
    rows, width = residual.shape
    experts = router_t.shape[0]
    wide = residual[...].astype(jnp.float32)
    mean_square = jnp.mean(wide * wide, axis=1, keepdims=True)
    scale = gain[...].reshape(1, width)
    normed = (wide * lax.rsqrt(mean_square + norm_eps) * scale).astype(jnp.bfloat16)
    here = station[0]
    lane_expert = lax.broadcasted_iota(jnp.int32, (experts, rows), 0) ^ here
    named_t = jnp.zeros((experts, rows), jnp.float32)
    for k in range(ids_t.shape[0]):
        named_t += jnp.where(ids_t[k : k + 1, :] == lane_expert, 1.0, 0.0)
    named_16 = named_t.astype(jnp.bfloat16)
    one = lax.broadcasted_iota(jnp.int32, (rows, rows), 0)
    two = lax.broadcasted_iota(jnp.int32, (rows, rows), 1)
    earlier_t = jnp.where(one < two, 1.0, 0.0).astype(jnp.bfloat16)
    slot_t = jnp.dot(named_16, earlier_t, preferred_element_type=jnp.float32)
    slot_t = jnp.where(named_t > 0.0, slot_t, -1.0)
    place = lax.broadcasted_iota(jnp.int32, (block_rows, rows), 0).astype(jnp.float32)
    for e in range(experts):
        hit = jnp.where(place == slot_t[e : e + 1, :], 1.0, 0.0).astype(jnp.bfloat16)
        block = jnp.dot(hit, normed, preferred_element_type=jnp.float32).astype(jnp.bfloat16)
        start = pl.multiple_of((here ^ e) * block_rows, 16)
        packed[pl.ds(start, block_rows), :] = block
    across = (((1,), (1,)), ((), ()))
    same = jnp.where(one == two, 1.0, 0.0).astype(jnp.bfloat16)
    earlier = jnp.where(two < one, 1.0, 0.0).astype(jnp.bfloat16)
    named = lax.dot_general(same, named_16, across, preferred_element_type=jnp.float32)
    slot = lax.dot_general(earlier, named_16, across, preferred_element_type=jnp.float32)
    slot = jnp.where(named > 0.0, slot, -1.0)
    logits = lax.dot_general(normed, router_t[...], across, preferred_element_type=jnp.float32)
    affinity = jax.nn.sigmoid(logits)
    column = lax.broadcasted_iota(jnp.int32, (rows, experts), 1)
    chosen = []
    for e in range(experts):
        value = jnp.sum(jnp.where(column == (here ^ e), affinity, 0.0), axis=1, keepdims=True)
        chosen.append(jnp.where(named[:, e : e + 1] > 0.0, value, 0.0))
    total = sum(chosen[1:], chosen[0])
    lanes = lax.broadcasted_iota(jnp.int32, (rows, table.shape[1]), 1)
    filled = jnp.zeros((rows, table.shape[1]), jnp.float32)
    for e in range(experts):
        filled = jnp.where(lanes == e, slot[:, e : e + 1], filled)
        filled = jnp.where(lanes == experts + e, route_scale * chosen[e] / total, filled)
    table[...] = filled


def prepare(residual, norm_gain, router, expert_ids, station, block_rows):
    rows, width = residual.shape
    experts = router.shape[1]
    whole = pl.BlockSpec(memory_space=pltpu.VMEM)
    return pl.pallas_call(
        functools.partial(prepare_kernel, block_rows),
        out_shape=[
            jax.ShapeDtypeStruct((rows, 128), jnp.float32),
            jax.ShapeDtypeStruct((experts * block_rows, width), jnp.bfloat16),
        ],
        in_specs=[pl.BlockSpec(memory_space=pltpu.SMEM)] + [whole] * 4,
        out_specs=[whole] * 2,
        compiler_params=pltpu.CompilerParams(vmem_limit_bytes=vmem_bytes),
    )(station[None], residual, norm_gain, router.T, expert_ids.T)


def moved(copies, sems):
    return [pltpu.make_async_copy(a, b, sems.at[i]) for i, (a, b) in enumerate(copies)]


def down_pieces(refs, target, copies, group, hidden, groups):
    pieces = []
    for ref, (member, shift, rows, column, columns) in zip(refs, copies):
        start = member * hidden
        if shift is not None:
            part = lax.rem(group + groups - shift, groups)
            start = pl.multiple_of(part * (hidden // groups) + start, 16)
        pieces.append((ref.at[:, pl.ds(column, columns)], target.at[pl.ds(start, rows), :]))
    return pieces


def down_product(act, wd, outs, first):
    block_rows = outs[0].shape[0]
    held = pl.ds(first * block_rows, len(outs) * block_rows)
    width = wd.shape[1]
    step = 256 if width % 256 == 0 else 128
    for base in range(0, width, step):
        span = pl.ds(base, step)
        value = jnp.dot(act[held, :], wd[:, span], preferred_element_type=jnp.float32)
        value = value.astype(jnp.bfloat16)
        for i, out in enumerate(outs):
            out[:, span] = value[i * block_rows : (i + 1) * block_rows, :]


def expert_kernel(plan, group, station, rows, *refs):
    block_rows, hidden, width, groups, weight_copies, down_copies = plan
    weight_refs, refs = refs[: len(weight_copies)], refs[len(weight_copies) :]
    down_refs, refs = refs[: len(down_copies)], refs[len(down_copies) :]
    act, outs, (x, w, wd, row_sems, weight_sems, down_sems) = refs[0], refs[1:-6], refs[-6:]
    members = w.shape[0]
    g = group[0]
    row_pieces = []
    for r in range(x.shape[0] // block_rows):
        start = pl.multiple_of((station[0] ^ r) * block_rows, 16)
        row_pieces.append(
            (rows.at[pl.ds(start, block_rows), :], x.at[pl.ds(r * block_rows, block_rows), :])
        )
    row_waits = moved(row_pieces, row_sems)
    stages = [[] for _ in range(members)]
    pieces = []
    for ref, (member, shift, base, size, column) in zip(weight_refs, weight_copies):
        start = base
        if shift is not None:
            part = lax.rem(g + groups - shift, groups)
            start = pl.multiple_of(part * (width // groups) + base, 16)
        pieces.append((ref, w.at[member, pl.ds(start, size), pl.ds(column, hidden)]))
    for copy, (member, *_) in zip(moved(pieces, weight_sems), weight_copies):
        stages[member].append(copy)
    stages.append(moved(down_pieces(down_refs, wd, down_copies, g, hidden, groups), down_sems))

    for copy in row_waits + stages[0]:
        copy.start()
    for copy in row_waits:
        copy.wait()
    for copy in stages[1]:
        copy.start()
    for member in range(members):
        for copy in stages[member]:
            copy.wait()
        if member + 2 <= members:
            for copy in stages[member + 2]:
                copy.start()
        gate = jnp.dot(x[...], w[member, :, :hidden], preferred_element_type=jnp.float32)
        up = jnp.dot(x[...], w[member, :, hidden:], preferred_element_type=jnp.float32)
        act[:, member * hidden : (member + 1) * hidden] = (
            gate / (1.0 + jnp.exp(-gate)) * up
        ).astype(jnp.bfloat16)
    for copy in stages[members]:
        copy.wait()
    down_product(act, wd, outs, x.shape[0] // block_rows - len(outs))


def expert_first(group, station, rows, weights, copies, downs, down_copies, sizes, members, done):
    block_rows, hidden, groups = sizes
    total_rows, width = rows.shape
    columns = down_copies[0][-1]
    blocks = total_rows // block_rows
    plan = (block_rows, hidden, width, groups, copies, down_copies)
    out = pl.pallas_call(
        functools.partial(expert_kernel, plan),
        out_shape=[jax.ShapeDtypeStruct((total_rows, members * hidden), jnp.bfloat16)]
        + [jax.ShapeDtypeStruct((block_rows, columns), jnp.bfloat16)] * done,
        in_specs=[pl.BlockSpec(memory_space=pltpu.SMEM)] * 2
        + [pl.BlockSpec(memory_space=pl.ANY)] * (1 + len(copies) + len(down_copies)),
        out_specs=[pl.BlockSpec(memory_space=pltpu.VMEM)] * (1 + done),
        scratch_shapes=[
            pltpu.VMEM((total_rows, width), jnp.bfloat16),
            pltpu.VMEM((members, width, 2 * hidden), jnp.bfloat16),
            pltpu.VMEM((members * hidden, columns), jnp.bfloat16),
            pltpu.SemaphoreType.DMA((blocks,)),
            pltpu.SemaphoreType.DMA((len(copies),)),
            pltpu.SemaphoreType.DMA((len(down_copies),)),
        ],
        compiler_params=pltpu.CompilerParams(vmem_limit_bytes=vmem_bytes),
    )(group, station, rows, *weights, *downs)
    return out[0], out[1:]


def down_kernel(plan, group, act, *refs):
    hidden, groups, copies = plan
    down_refs, outs, (wd, sems) = refs[: len(copies)], refs[len(copies) : -2], refs[-2:]
    waits = moved(down_pieces(down_refs, wd, copies, group[0], hidden, groups), sems)
    for copy in waits:
        copy.start()
    for copy in waits:
        copy.wait()
    down_product(act, wd, outs, 0)


def expert_later(group, act, downs, copies, sizes, blocks):
    block_rows, hidden, groups = sizes
    columns = copies[0][-1]
    whole = pl.BlockSpec(memory_space=pltpu.VMEM)
    return pl.pallas_call(
        functools.partial(down_kernel, (hidden, groups, copies)),
        out_shape=[jax.ShapeDtypeStruct((block_rows, columns), jnp.bfloat16)] * blocks,
        in_specs=[pl.BlockSpec(memory_space=pltpu.SMEM), whole]
        + [pl.BlockSpec(memory_space=pl.ANY)] * len(downs),
        out_specs=[whole] * blocks,
        scratch_shapes=[
            pltpu.VMEM((act.shape[1], columns), jnp.bfloat16),
            pltpu.SemaphoreType.DMA((len(copies),)),
        ],
        compiler_params=pltpu.CompilerParams(vmem_limit_bytes=late_vmem_bytes),
    )(group, act, *downs)


def lanes_for(count):
    return -(-count // 128) * 128


def weighted_sum(plan, is_hub, table, blocks, high, low):
    classes, experts = plan
    block_rows = blocks[0].shape[0]
    rows = table.shape[0]
    used = pl.ds(0, block_rows * len(blocks))
    place = lax.broadcasted_iota(jnp.int32, (rows, block_rows), 1).astype(jnp.float32)
    for i, (e, at_hub) in enumerate(classes):
        gate = table[:, experts + e : experts + e + 1]
        if not at_hub:
            gate = jnp.where(is_hub[0] == 1, 0.0, gate)
        weight = jnp.where(place == table[:, e : e + 1], gate, 0.0)
        upper = weight.astype(jnp.bfloat16)
        columns = pl.ds(i * block_rows, block_rows)
        high[:, columns] = upper
        low[:, columns] = (weight - upper.astype(jnp.float32)).astype(jnp.bfloat16)
    stacked = jnp.concatenate([block[...] for block in blocks], axis=0)
    total = jnp.dot(high[:, used], stacked, preferred_element_type=jnp.float32)
    return total + jnp.dot(low[:, used], stacked, preferred_element_type=jnp.float32)


def partner_kernel(plan, is_hub, table, *refs):
    blocks, (out, high, low) = refs[:-3], refs[-3:]
    out[...] = weighted_sum(plan, is_hub, table, blocks, high, low).astype(jnp.bfloat16)


def partner_sum(plan, is_hub, table, blocks):
    block_rows, width = blocks[0].shape
    rows = table.shape[0]
    whole = pl.BlockSpec(memory_space=pltpu.VMEM)
    return pl.pallas_call(
        functools.partial(partner_kernel, plan),
        out_shape=jax.ShapeDtypeStruct((rows, width), jnp.bfloat16),
        in_specs=[pl.BlockSpec(memory_space=pltpu.SMEM)] + [whole] * (1 + len(blocks)),
        out_specs=whole,
        scratch_shapes=[pltpu.VMEM((rows, lanes_for(block_rows * len(blocks))), jnp.bfloat16)] * 2,
        compiler_params=pltpu.CompilerParams(vmem_limit_bytes=late_vmem_bytes),
    )(is_hub, table, *blocks)


def result_kernel(plan, is_hub, table, *refs):
    sum_plan, base, size = plan
    count = len(sum_plan[0])
    blocks = refs[:count]
    hub_sum, residual = refs[count : count + 2]
    out, high, low, held, result, sems = refs[-6:]
    span = pl.ds(base, size)
    fetch = pltpu.make_async_copy(residual.at[:, span], held, sems.at[0])
    fetch.start()
    total = weighted_sum(sum_plan, is_hub, table, blocks, high, low)
    fetch.wait()
    total += held[...].astype(jnp.float32) + hub_sum[...].astype(jnp.float32)
    result[...] = total.astype(jnp.bfloat16)
    store = pltpu.make_async_copy(result, out.at[:, span], sems.at[1])
    store.start()
    store.wait()


def result(plan, is_hub, table, blocks, hub_sum, residual, base, size, so_far):
    block_rows = blocks[0].shape[0]
    rows, width = residual.shape
    whole = pl.BlockSpec(memory_space=pltpu.VMEM)
    anywhere = pl.BlockSpec(memory_space=pl.ANY)
    first = so_far is None
    earlier = [] if first else [so_far]
    return pl.pallas_call(
        functools.partial(result_kernel, (plan, base, size)),
        out_shape=jax.ShapeDtypeStruct((rows, width), jnp.bfloat16),
        in_specs=[pl.BlockSpec(memory_space=pltpu.SMEM)]
        + [whole] * (2 + len(blocks))
        + [anywhere] * (1 + len(earlier)),
        out_specs=anywhere,
        scratch_shapes=[pltpu.VMEM((rows, lanes_for(block_rows * len(blocks))), jnp.bfloat16)] * 2
        + [pltpu.VMEM((rows, size), jnp.bfloat16)] * 2
        + [pltpu.SemaphoreType.DMA((2,))],
        input_output_aliases={} if first else {len(blocks) + 4: 0},
        compiler_params=pltpu.CompilerParams(vmem_limit_bytes=late_vmem_bytes),
    )(is_hub, table, *blocks, hub_sum, residual, *earlier)


def named(name, function, *args):
    with jax.named_scope(name):
        return function(*args)


def after(value, *others):
    return lax.optimization_barrier((value,) + others)[0]


def shards(residual, norm_gain, router, w_gate, w_up, w_down, expert_ids):
    tok_rows, width = residual.shape
    top = expert_ids.shape[1]
    experts = router.shape[1]
    device_count = lax.axis_size("expert")
    groups = lax.axis_size("groups")
    members = device_count // experts
    hidden = w_gate.shape[1]
    capacity = 3 * tok_rows * top // (2 * experts)
    block_rows = -(-capacity // 16) * 16
    my_group = lax.axis_index("groups")
    station = (lax.axis_index("expert") // members).astype(jnp.int32)
    half = experts // 2
    last = experts - 1
    hubs = (half - 1, half)
    is_hub = jnp.logical_or(station == hubs[0], station == hubs[1]).astype(jnp.int32)[None]

    def along(value, route):
        pairs = [
            (a * members + m, b * members + m) for a, b in route.items() for m in range(members)
        ]
        return lax.ppermute(value, "expert", pairs)

    near = {r: {z: z ^ r for z in range(experts)} for r in range(1, half)}
    mixed = {
        r: {z: z ^ (r ^ last if z in hubs else r) for z in range(experts)}
        for r in range(half, last)
    }
    far = {z: z ^ last for z in range(experts) if z not in hubs}
    between = {hubs[0]: hubs[1], hubs[1]: hubs[0]}

    part_width, part_hidden = width // groups, hidden // groups
    jobs = []
    for distance in range(2, members, 2):
        for i, w in enumerate((w_gate, w_up)):
            early = part_width // ((first_share if i == 0 else 2) * 16) * 16
            for base, size in ((0, early), (early, part_width - early)):
                sent = lax.dynamic_slice_in_dim(w, my_group * part_width + base, size, 0)
                jobs.append((sent, distance, (base, size, i * hidden), None))
    columns = cuts(width, down_chunks, 128)
    for c, (base, size) in enumerate(columns):
        for distance in range(2, members, 2):
            sent = lax.dynamic_slice(w_down, (my_group * part_hidden, base), (part_hidden, size))
            jobs.append((sent, distance, None, c))
    table, packed = prepare(after(residual, jobs[0][0]), norm_gain, router, expert_ids, station, block_rows)
    lines = [[e * members + m for e in range(experts)] for m in range(members)]
    hub_table = named("table", along, table, between)

    last_job = len(jobs) - 1
    group = my_group[None].astype(jnp.int32)
    weights = [w_gate, w_up] + [named("own", flipped, w, 1) for w in (w_gate, w_up)]
    copies = [(m, None, 0, width, i * hidden) for m in range(2) for i in range(2)]
    own_down = named("own", flipped, w_down, 1)
    downs = [[w_down, own_down] for _ in columns]
    down_copies = [[(m, None, hidden, base, size) for m in range(2)] for base, size in columns]
    Y, X = [], []
    rows = None
    for n, (sent, distance, gate_up, chunk) in enumerate(jobs):
        Y.append(named(f"Y{n}", flipped, after(sent, *Y[-1:], *(X[-2] if n > 1 else [])), distance))
        if n == 0:
            packed = after(packed, Y[0], hub_table)
            rows = lax.all_to_all(packed, "expert", 0, 0, axis_index_groups=lines, tiled=True)
        ready = after(Y[n], *X[-1]) if X else Y[n]
        X.append([named(f"X{n}", turned, ready, shift) for shift in range(1, groups)])
    sizes = (block_rows, hidden, groups)
    first_jobs = sum(1 for job in jobs if job[3] in (None, 0))
    act = None
    for n, (sent, distance, gate_up, chunk) in enumerate(jobs):
        if n == first_jobs:
            act, first_outs = expert_first(
                group, station[None], rows, weights, copies, downs[0], down_copies[0], sizes, members, half
            )
        for offset in range(2):
            for shift, part in enumerate([Y[n]] + X[n]):
                if offset:
                    part = named(f"C{n}", flipped, part if act is None else after(part, act), 1)
                if gate_up is not None:
                    base, size, column = gate_up
                    weights.append(part)
                    copies.append((distance + offset, shift, base, size, column))
                else:
                    downs[chunk].append(part)
                    down_copies[chunk].append(
                        (distance + offset, shift, part_hidden, 0, columns[chunk][1])
                    )

    partner = [(r, True) for r in mixed] + [(last, True)]
    classes = [(r, r < half) for r in range(experts)]
    layer_out = None
    for c, (base, size) in enumerate(columns):
        count = half if c == 0 else experts
        outs = list(expert_later(group, act, downs[c], down_copies[c], sizes, count))
        if c == 0:
            outs += first_outs
        back = [outs[0]] + [None] * last
        for r in mixed:
            route = {b: a for a, b in mixed[r].items()}
            back[r] = named(f"mixed_back{c}", along, outs[r], route)
        back[last] = named(f"far_back{c}", along, outs[last], far)
        for r in near:
            back[r] = named(f"near_back{c}", along, outs[r], near[r])
        held = [back[r] for r in mixed] + [outs[last]]
        hub_sum = partner_sum((partner, experts), is_hub, hub_table, held)
        hub_sum = named(f"sum_back{c}", along, hub_sum, between)
        layer_out = result(
            (classes, experts), is_hub, table, back, hub_sum, residual, base, size, layer_out
        )
    return layer_out


def solution(mesh):
    in_specs = (
        P(("groups", "expert"), None),
        P(),
        P(),
        P(None, "expert"),
        P(None, "expert"),
        P("expert", None),
        P(("groups", "expert"), None),
    )
    out_specs = P(("groups", "expert"), None)
    return jax.shard_map(shards, mesh=mesh, in_specs=in_specs, out_specs=out_specs, check_vma=False)
```

```python
import functools

import jax
import jax.numpy as jnp
from jax import lax
from jax.experimental import pallas as pl
from jax.experimental.pallas import tpu as pltpu
from jax.sharding import PartitionSpec as P

route_scale = 2.5
norm_eps = 1e-06
first_share = 2
down_chunks = 2
vmem_bytes = 56 * 1024 * 1024
late_vmem_bytes = 24 * 1024 * 1024


def flipped(value, distance):
    pairs = [(source, source ^ distance) for source in range(lax.axis_size("expert"))]
    return lax.ppermute(value, "expert", pairs)


def turned(value, shift):
    count = lax.axis_size("groups")
    pairs = [(source, (source + shift) % count) for source in range(count)]
    return lax.ppermute(value, "groups", pairs)


def cuts(total, count, unit):
    marks = [total // unit * i // count * unit for i in range(count)] + [total]
    return [(low, high - low) for low, high in zip(marks[:-1], marks[1:])]


def prepare_kernel(block_rows, station, residual, gain, router_t, ids_t, table, packed):
    rows, width = residual.shape
    experts = router_t.shape[0]
    wide = residual[...].astype(jnp.float32)
    mean_square = jnp.mean(wide * wide, axis=1, keepdims=True)
    scale = gain[...].reshape(1, width)
    normed = (wide * lax.rsqrt(mean_square + norm_eps) * scale).astype(jnp.bfloat16)
    here = station[0]
    lane_expert = lax.broadcasted_iota(jnp.int32, (experts, rows), 0) ^ here
    named_t = jnp.zeros((experts, rows), jnp.float32)
    for k in range(ids_t.shape[0]):
        named_t += jnp.where(ids_t[k : k + 1, :] == lane_expert, 1.0, 0.0)
    named_16 = named_t.astype(jnp.bfloat16)
    one = lax.broadcasted_iota(jnp.int32, (rows, rows), 0)
    two = lax.broadcasted_iota(jnp.int32, (rows, rows), 1)
    earlier_t = jnp.where(one < two, 1.0, 0.0).astype(jnp.bfloat16)
    slot_t = jnp.dot(named_16, earlier_t, preferred_element_type=jnp.float32)
    slot_t = jnp.where(named_t > 0.0, slot_t, -1.0)
    place = lax.broadcasted_iota(jnp.int32, (block_rows, rows), 0).astype(jnp.float32)
    for e in range(experts):
        hit = jnp.where(place == slot_t[e : e + 1, :], 1.0, 0.0).astype(jnp.bfloat16)
        block = jnp.dot(hit, normed, preferred_element_type=jnp.float32).astype(jnp.bfloat16)
        start = pl.multiple_of((here ^ e) * block_rows, 16)
        packed[pl.ds(start, block_rows), :] = block
    across = (((1,), (1,)), ((), ()))
    same = jnp.where(one == two, 1.0, 0.0).astype(jnp.bfloat16)
    earlier = jnp.where(two < one, 1.0, 0.0).astype(jnp.bfloat16)
    named = lax.dot_general(same, named_16, across, preferred_element_type=jnp.float32)
    slot = lax.dot_general(earlier, named_16, across, preferred_element_type=jnp.float32)
    slot = jnp.where(named > 0.0, slot, -1.0)
    logits = lax.dot_general(normed, router_t[...], across, preferred_element_type=jnp.float32)
    affinity = jax.nn.sigmoid(logits)
    column = lax.broadcasted_iota(jnp.int32, (rows, experts), 1)
    chosen = []
    for e in range(experts):
        value = jnp.sum(jnp.where(column == (here ^ e), affinity, 0.0), axis=1, keepdims=True)
        chosen.append(jnp.where(named[:, e : e + 1] > 0.0, value, 0.0))
    total = sum(chosen[1:], chosen[0])
    lanes = lax.broadcasted_iota(jnp.int32, (rows, table.shape[1]), 1)
    filled = jnp.zeros((rows, table.shape[1]), jnp.float32)
    for e in range(experts):
        filled = jnp.where(lanes == e, slot[:, e : e + 1], filled)
        filled = jnp.where(lanes == experts + e, route_scale * chosen[e] / total, filled)
    table[...] = filled


def prepare(residual, norm_gain, router, expert_ids, station, block_rows):
    rows, width = residual.shape
    experts = router.shape[1]
    whole = pl.BlockSpec(memory_space=pltpu.VMEM)
    return pl.pallas_call(
        functools.partial(prepare_kernel, block_rows),
        out_shape=[
            jax.ShapeDtypeStruct((rows, 128), jnp.float32),
            jax.ShapeDtypeStruct((experts * block_rows, width), jnp.bfloat16),
        ],
        in_specs=[pl.BlockSpec(memory_space=pltpu.SMEM)] + [whole] * 4,
        out_specs=[whole] * 2,
        compiler_params=pltpu.CompilerParams(vmem_limit_bytes=vmem_bytes),
    )(station[None], residual, norm_gain, router.T, expert_ids.T)


def moved(copies, sems):
    return [pltpu.make_async_copy(a, b, sems.at[i]) for i, (a, b) in enumerate(copies)]


def down_pieces(refs, target, copies, group, hidden, groups):
    pieces = []
    for ref, (member, shift, rows, column, columns) in zip(refs, copies):
        start = member * hidden
        if shift is not None:
            part = lax.rem(group + groups - shift, groups)
            start = pl.multiple_of(part * (hidden // groups) + start, 16)
        pieces.append((ref.at[:, pl.ds(column, columns)], target.at[pl.ds(start, rows), :]))
    return pieces


def down_product(act, wd, outs, first):
    block_rows = outs[0].shape[0]
    held = pl.ds(first * block_rows, len(outs) * block_rows)
    width = wd.shape[1]
    step = 256 if width % 256 == 0 else 128
    for base in range(0, width, step):
        span = pl.ds(base, step)
        value = jnp.dot(act[held, :], wd[:, span], preferred_element_type=jnp.float32)
        value = value.astype(jnp.bfloat16)
        for i, out in enumerate(outs):
            out[:, span] = value[i * block_rows : (i + 1) * block_rows, :]


def expert_kernel(plan, group, station, rows, *refs):
    block_rows, hidden, width, groups, weight_copies, down_copies = plan
    weight_refs, refs = refs[: len(weight_copies)], refs[len(weight_copies) :]
    down_refs, refs = refs[: len(down_copies)], refs[len(down_copies) :]
    act, outs, (x, w, wd, row_sems, weight_sems, down_sems) = refs[0], refs[1:-6], refs[-6:]
    members = w.shape[0]
    g = group[0]
    row_pieces = []
    for r in range(x.shape[0] // block_rows):
        start = pl.multiple_of((station[0] ^ r) * block_rows, 16)
        row_pieces.append(
            (rows.at[pl.ds(start, block_rows), :], x.at[pl.ds(r * block_rows, block_rows), :])
        )
    row_waits = moved(row_pieces, row_sems)
    stages = [[] for _ in range(members)]
    pieces = []
    for ref, (member, shift, base, size, column) in zip(weight_refs, weight_copies):
        start = base
        if shift is not None:
            part = lax.rem(g + groups - shift, groups)
            start = pl.multiple_of(part * (width // groups) + base, 16)
        pieces.append((ref, w.at[member, pl.ds(start, size), pl.ds(column, hidden)]))
    for copy, (member, *_) in zip(moved(pieces, weight_sems), weight_copies):
        stages[member].append(copy)
    stages.append(moved(down_pieces(down_refs, wd, down_copies, g, hidden, groups), down_sems))

    for copy in row_waits + stages[0]:
        copy.start()
    for copy in row_waits:
        copy.wait()
    for copy in stages[1]:
        copy.start()
    for member in range(members):
        for copy in stages[member]:
            copy.wait()
        if member + 2 <= members:
            for copy in stages[member + 2]:
                copy.start()
        gate = jnp.dot(x[...], w[member, :, :hidden], preferred_element_type=jnp.float32)
        up = jnp.dot(x[...], w[member, :, hidden:], preferred_element_type=jnp.float32)
        act[:, member * hidden : (member + 1) * hidden] = (
            gate / (1.0 + jnp.exp(-gate)) * up
        ).astype(jnp.bfloat16)
    for copy in stages[members]:
        copy.wait()
    down_product(act, wd, outs, x.shape[0] // block_rows - len(outs))


def expert_first(group, station, rows, weights, copies, downs, down_copies, sizes, members, done):
    block_rows, hidden, groups = sizes
    total_rows, width = rows.shape
    columns = down_copies[0][-1]
    blocks = total_rows // block_rows
    plan = (block_rows, hidden, width, groups, copies, down_copies)
    out = pl.pallas_call(
        functools.partial(expert_kernel, plan),
        out_shape=[jax.ShapeDtypeStruct((total_rows, members * hidden), jnp.bfloat16)]
        + [jax.ShapeDtypeStruct((block_rows, columns), jnp.bfloat16)] * done,
        in_specs=[pl.BlockSpec(memory_space=pltpu.SMEM)] * 2
        + [pl.BlockSpec(memory_space=pl.ANY)] * (1 + len(copies) + len(down_copies)),
        out_specs=[pl.BlockSpec(memory_space=pltpu.VMEM)] * (1 + done),
        scratch_shapes=[
            pltpu.VMEM((total_rows, width), jnp.bfloat16),
            pltpu.VMEM((members, width, 2 * hidden), jnp.bfloat16),
            pltpu.VMEM((members * hidden, columns), jnp.bfloat16),
            pltpu.SemaphoreType.DMA((blocks,)),
            pltpu.SemaphoreType.DMA((len(copies),)),
            pltpu.SemaphoreType.DMA((len(down_copies),)),
        ],
        compiler_params=pltpu.CompilerParams(vmem_limit_bytes=vmem_bytes),
    )(group, station, rows, *weights, *downs)
    return out[0], out[1:]


def down_kernel(plan, group, act, *refs):
    hidden, groups, copies = plan
    down_refs, outs, (wd, sems) = refs[: len(copies)], refs[len(copies) : -2], refs[-2:]
    waits = moved(down_pieces(down_refs, wd, copies, group[0], hidden, groups), sems)
    for copy in waits:
        copy.start()
    for copy in waits:
        copy.wait()
    down_product(act, wd, outs, 0)


def expert_later(group, act, downs, copies, sizes, blocks):
    block_rows, hidden, groups = sizes
    columns = copies[0][-1]
    whole = pl.BlockSpec(memory_space=pltpu.VMEM)
    return pl.pallas_call(
        functools.partial(down_kernel, (hidden, groups, copies)),
        out_shape=[jax.ShapeDtypeStruct((block_rows, columns), jnp.bfloat16)] * blocks,
        in_specs=[pl.BlockSpec(memory_space=pltpu.SMEM), whole]
        + [pl.BlockSpec(memory_space=pl.ANY)] * len(downs),
        out_specs=[whole] * blocks,
        scratch_shapes=[
            pltpu.VMEM((act.shape[1], columns), jnp.bfloat16),
            pltpu.SemaphoreType.DMA((len(copies),)),
        ],
        compiler_params=pltpu.CompilerParams(vmem_limit_bytes=late_vmem_bytes),
    )(group, act, *downs)


def lanes_for(count):
    return -(-count // 128) * 128


def weighted_sum(plan, is_hub, table, blocks, high, low):
    classes, experts = plan
    block_rows = blocks[0].shape[0]
    rows = table.shape[0]
    used = pl.ds(0, block_rows * len(blocks))
    place = lax.broadcasted_iota(jnp.int32, (rows, block_rows), 1).astype(jnp.float32)
    for i, (e, at_hub) in enumerate(classes):
        gate = table[:, experts + e : experts + e + 1]
        if not at_hub:
            gate = jnp.where(is_hub[0] == 1, 0.0, gate)
        weight = jnp.where(place == table[:, e : e + 1], gate, 0.0)
        upper = weight.astype(jnp.bfloat16)
        columns = pl.ds(i * block_rows, block_rows)
        high[:, columns] = upper
        low[:, columns] = (weight - upper.astype(jnp.float32)).astype(jnp.bfloat16)
    stacked = jnp.concatenate([block[...] for block in blocks], axis=0)
    total = jnp.dot(high[:, used], stacked, preferred_element_type=jnp.float32)
    return total + jnp.dot(low[:, used], stacked, preferred_element_type=jnp.float32)


def partner_kernel(plan, is_hub, table, *refs):
    blocks, (out, high, low) = refs[:-3], refs[-3:]
    out[...] = weighted_sum(plan, is_hub, table, blocks, high, low).astype(jnp.bfloat16)


def partner_sum(plan, is_hub, table, blocks):
    block_rows, width = blocks[0].shape
    rows = table.shape[0]
    whole = pl.BlockSpec(memory_space=pltpu.VMEM)
    return pl.pallas_call(
        functools.partial(partner_kernel, plan),
        out_shape=jax.ShapeDtypeStruct((rows, width), jnp.bfloat16),
        in_specs=[pl.BlockSpec(memory_space=pltpu.SMEM)] + [whole] * (1 + len(blocks)),
        out_specs=whole,
        scratch_shapes=[pltpu.VMEM((rows, lanes_for(block_rows * len(blocks))), jnp.bfloat16)] * 2,
        compiler_params=pltpu.CompilerParams(vmem_limit_bytes=late_vmem_bytes),
    )(is_hub, table, *blocks)


def result_kernel(plan, is_hub, table, *refs):
    sum_plan, base, size = plan
    count = len(sum_plan[0])
    blocks = refs[:count]
    hub_sum, residual = refs[count : count + 2]
    out, high, low, held, result, sems = refs[-6:]
    span = pl.ds(base, size)
    fetch = pltpu.make_async_copy(residual.at[:, span], held, sems.at[0])
    fetch.start()
    total = weighted_sum(sum_plan, is_hub, table, blocks, high, low)
    fetch.wait()
    total += held[...].astype(jnp.float32) + hub_sum[...].astype(jnp.float32)
    result[...] = total.astype(jnp.bfloat16)
    store = pltpu.make_async_copy(result, out.at[:, span], sems.at[1])
    store.start()
    store.wait()


def result(plan, is_hub, table, blocks, hub_sum, residual, base, size, so_far):
    block_rows = blocks[0].shape[0]
    rows, width = residual.shape
    whole = pl.BlockSpec(memory_space=pltpu.VMEM)
    anywhere = pl.BlockSpec(memory_space=pl.ANY)
    first = so_far is None
    earlier = [] if first else [so_far]
    return pl.pallas_call(
        functools.partial(result_kernel, (plan, base, size)),
        out_shape=jax.ShapeDtypeStruct((rows, width), jnp.bfloat16),
        in_specs=[pl.BlockSpec(memory_space=pltpu.SMEM)]
        + [whole] * (2 + len(blocks))
        + [anywhere] * (1 + len(earlier)),
        out_specs=anywhere,
        scratch_shapes=[pltpu.VMEM((rows, lanes_for(block_rows * len(blocks))), jnp.bfloat16)] * 2
        + [pltpu.VMEM((rows, size), jnp.bfloat16)] * 2
        + [pltpu.SemaphoreType.DMA((2,))],
        input_output_aliases={} if first else {len(blocks) + 4: 0},
        compiler_params=pltpu.CompilerParams(vmem_limit_bytes=late_vmem_bytes),
    )(is_hub, table, *blocks, hub_sum, residual, *earlier)


def named(name, function, *args):
    with jax.named_scope(name):
        return function(*args)


def after(value, *others):
    return lax.optimization_barrier((value,) + others)[0]


def shards(residual, norm_gain, router, w_gate, w_up, w_down, expert_ids):
    tok_rows, width = residual.shape
    top = expert_ids.shape[1]
    experts = router.shape[1]
    device_count = lax.axis_size("expert")
    groups = lax.axis_size("groups")
    members = device_count // experts
    hidden = w_gate.shape[1]
    capacity = 3 * tok_rows * top // (2 * experts)
    block_rows = -(-capacity // 16) * 16
    my_group = lax.axis_index("groups")
    station = (lax.axis_index("expert") // members).astype(jnp.int32)
    half = experts // 2
    last = experts - 1
    hubs = (half - 1, half)
    is_hub = jnp.logical_or(station == hubs[0], station == hubs[1]).astype(jnp.int32)[None]

    def along(value, route):
        pairs = [
            (a * members + m, b * members + m) for a, b in route.items() for m in range(members)
        ]
        return lax.ppermute(value, "expert", pairs)

    near = {r: {z: z ^ r for z in range(experts)} for r in range(1, half)}
    mixed = {
        r: {z: z ^ (r ^ last if z in hubs else r) for z in range(experts)}
        for r in range(half, last)
    }
    far = {z: z ^ last for z in range(experts) if z not in hubs}
    between = {hubs[0]: hubs[1], hubs[1]: hubs[0]}

    part_width, part_hidden = width // groups, hidden // groups
    jobs = []
    for distance in range(2, members, 2):
        for i, w in enumerate((w_gate, w_up)):
            early = part_width // ((first_share if i == 0 else 2) * 16) * 16
            for base, size in ((0, early), (early, part_width - early)):
                sent = lax.dynamic_slice_in_dim(w, my_group * part_width + base, size, 0)
                jobs.append((sent, distance, (base, size, i * hidden), None))
    columns = cuts(width, down_chunks, 128)
    for c, (base, size) in enumerate(columns):
        for distance in range(2, members, 2):
            sent = lax.dynamic_slice(w_down, (my_group * part_hidden, base), (part_hidden, size))
            jobs.append((sent, distance, None, c))
    table, packed = prepare(after(residual, jobs[0][0]), norm_gain, router, expert_ids, station, block_rows)
    lines = [[e * members + m for e in range(experts)] for m in range(members)]
    hub_table = named("table", along, table, between)

    last_job = len(jobs) - 1
    group = my_group[None].astype(jnp.int32)
    weights = [w_gate, w_up] + [named("own", flipped, w, 1) for w in (w_gate, w_up)]
    copies = [(m, None, 0, width, i * hidden) for m in range(2) for i in range(2)]
    own_down = named("own", flipped, w_down, 1)
    downs = [[w_down, own_down] for _ in columns]
    down_copies = [[(m, None, hidden, base, size) for m in range(2)] for base, size in columns]
    Y, X = [], []
    rows = None
    for n, (sent, distance, gate_up, chunk) in enumerate(jobs):
        Y.append(named(f"Y{n}", flipped, after(sent, *Y[-1:], *(X[-3] if n > 2 else [])), distance))
        if n == 0:
            packed = after(packed, Y[0], hub_table)
            rows = lax.all_to_all(packed, "expert", 0, 0, axis_index_groups=lines, tiled=True)
        ready = after(Y[n], *X[-1]) if X else Y[n]
        X.append([named(f"X{n}", turned, ready, shift) for shift in range(1, groups)])
    sizes = (block_rows, hidden, groups)
    first_jobs = sum(1 for job in jobs if job[3] in (None, 0))
    act = None
    for n, (sent, distance, gate_up, chunk) in enumerate(jobs):
        if n == first_jobs:
            act, first_outs = expert_first(
                group, station[None], rows, weights, copies, downs[0], down_copies[0], sizes, members, half
            )
        for offset in range(2):
            for shift, part in enumerate([Y[n]] + X[n]):
                if offset:
                    part = named(f"C{n}", flipped, part if act is None else after(part, act), 1)
                if gate_up is not None:
                    base, size, column = gate_up
                    weights.append(part)
                    copies.append((distance + offset, shift, base, size, column))
                else:
                    downs[chunk].append(part)
                    down_copies[chunk].append(
                        (distance + offset, shift, part_hidden, 0, columns[chunk][1])
                    )

    partner = [(r, True) for r in mixed] + [(last, True)]
    classes = [(r, r < half) for r in range(experts)]
    layer_out = None
    for c, (base, size) in enumerate(columns):
        count = half if c == 0 else experts
        outs = list(expert_later(group, act, downs[c], down_copies[c], sizes, count))
        if c == 0:
            outs += first_outs
        back = [outs[0]] + [None] * last
        for r in mixed:
            route = {b: a for a, b in mixed[r].items()}
            back[r] = named(f"mixed_back{c}", along, outs[r], route)
        back[last] = named(f"far_back{c}", along, outs[last], far)
        for r in near:
            back[r] = named(f"near_back{c}", along, outs[r], near[r])
        held = [back[r] for r in mixed] + [outs[last]]
        hub_sum = partner_sum((partner, experts), is_hub, hub_table, held)
        hub_sum = named(f"sum_back{c}", along, hub_sum, between)
        layer_out = result(
            (classes, experts), is_hub, table, back, hub_sum, residual, base, size, layer_out
        )
    return layer_out


def solution(mesh):
    in_specs = (
        P(("groups", "expert"), None),
        P(),
        P(),
        P(None, "expert"),
        P(None, "expert"),
        P("expert", None),
        P(("groups", "expert"), None),
    )
    out_specs = P(("groups", "expert"), None)
    return jax.shard_map(shards, mesh=mesh, in_specs=in_specs, out_specs=out_specs, check_vma=False)
```
